256 devices in a mesh: dp: 8 (over x_hi, y), ctx: 32 (over z, x_lo, core).
Axes of the slice: x: 4 (x_hi: 2, x_lo: 2; x = x_hi * 2 + x_lo), y: 4, z: 8, core: 2. Of those that a mesh axis runs over, the one named last changes fastest.
Arguments:
- queries: bfloat16 [65536, 4096], P(('dp', 'ctx')), may hold values from -5 to 5
- conv_keys: bfloat16 [65536, 512], P(('dp', 'ctx')), may hold values from -5 to 5
- conv_values: bfloat16 [65536, 512], P(('dp', 'ctx')), may hold values from -5 to 5
- out_grad: bfloat16 [65536, 4096], P(('dp', 'ctx')), may hold values from -5 to 5
- segment_ids: int32 [256, 256], P(('dp', 'ctx')), may hold values from 0 to 2, never falling along the last dimension, each value on 1 to 128 neighbouring positions
- cart_keys: bfloat16 [1024, 512], P('ctx'), may hold values from -5 to 5
- cart_values: bfloat16 [1024, 512], P('ctx'), may hold values from -5 to 5
Outputs:
- cart_key_grad: float32 [1024, 512], P('ctx')
- cart_value_grad: float32 [1024, 512], P('ctx')
The draws below stay inside these ranges and needn't reach their ends.
Inputs may be any that keep to these rules, and one draw needn't show every extreme that they name: `segment_ids`: within a block the numbers never fall; each block holds 3 conversations of 1 to 128 tokens, one of exactly 128.
All inputs are finite; a program needn't handle non-finite values.
Results may differ from the reference program's by a relative error of at most 0.0041.
Values may be sent and summed in bfloat16 or wider, within the bound.
No kernel may reach another device: no remote copies, remote signals or barrier semaphores. Data moves between devices by JAX's collectives and lax.ppermute only.
A program may use at most 128 MiB of HBM per device.

```python
import math
import jax
import jax.numpy as jnp
import numpy as np
from jax import lax

HQ = 32
HK = 4
HD = 128
TOK_DEV = 256
BLOCKS = 256
TOKENS = 65536
CART = 1024


def draw_cart_keys(key, part):
    key = jax.random.fold_in(key, 11)
    result = jnp.clip(jax.random.normal(key, (CART, HK * HD), jnp.float32), -5.0, 5.0)
    return result.astype(jnp.bfloat16)


def draw_queries(key, part):
    key = jax.random.fold_in(key, 23)
    result = jnp.clip(jax.random.normal(key, (TOKENS, HQ * HD), jnp.float32), -5.0, 5.0)
    return result.astype(jnp.bfloat16)


def shard_levels(rng, dims, shards, least, largest):
    level = 1.0
    for dim, shards_of in shards:
        draws = jax.random.uniform(jax.random.fold_in(jax.random.fold_in(rng, 6), dim), (shards_of,), jnp.float32, least / len(shards), largest / len(shards))
        level = level * jnp.repeat(jnp.exp(draws), dims[dim] // shards_of).reshape((-1,) + (1,) * (len(dims) - 1 - dim))
    return level


def split_up(number_of, total, bound, lean):
    portions = [(1 << 20) // math.isqrt(standing ** lean) + 1 for standing in range(2, number_of + 1)]
    surplus, counts = total - bound - (number_of - 1), [1] * (number_of - 1)
    while surplus > 0:
        candidates = [i for i in range(number_of - 1) if counts[i] < bound]
        pool, remaining = sum([portions[i] for i in candidates]), surplus
        for i in candidates:
            more = min(bound - counts[i], max(1, remaining * portions[i] // pool), surplus)
            counts[i] = counts[i] + more
            surplus = surplus - more
    return np.array([bound] + counts)


def ragged(stream_key, amount, total, limit, lean):
    if amount == 2:
        one = jax.random.randint(stream_key, (), max(1, total - limit), min(limit, total - 1) + 1)
        return jnp.stack([one, total - one])
    sizes = jnp.asarray(split_up(amount, total, limit, lean), jnp.int32)
    pairs = (amount - 1) // 2
    donor, receiver = sizes[1:1 + 2 * pairs:2], sizes[2:2 + 2 * pairs:2]
    room = jnp.minimum(donor - 1, limit - receiver)
    passed = jax.random.randint(jax.random.fold_in(stream_key, 1), (pairs,), 0, 1 << 20) % (room + 1)
    sizes = sizes.at[1:1 + 2 * pairs:2].set(donor - passed).at[2:2 + 2 * pairs:2].set(receiver + passed)
    return sizes[jax.random.permutation(jax.random.fold_in(stream_key, 2), amount)]


def noise(own_key, shape, width, bound, split=(), dtype=jnp.bfloat16):
    entries = width * jax.random.normal(own_key, shape, jnp.float32)
    if split:
        entries = entries * shard_levels(own_key, shape, split, -0.22, 0.18)
    return jnp.clip(entries, -bound, bound).astype(dtype)


def setup_inputs(seed: int = 0) -> dict:
    seeds = jax.random.split(jax.random.key(seed), 8)
    queries = draw_queries(jax.random.fold_in(seeds[7], 71), 0)
    conv_keys = noise(seeds[1], (TOKENS, HK * HD), 1.0, 5.0, ((0, 256),))
    conv_values = noise(seeds[2], (TOKENS, HK * HD), 1.0, 5.0, ((0, 256),))
    out_grad = noise(seeds[3], (TOKENS, HQ * HD), 1.0, 5.0, ((0, 256),))
    segment_ids = jax.vmap(lambda own: jnp.searchsorted(jnp.cumsum(ragged(own, 3, TOK_DEV, TOK_DEV // 2, 0)), jnp.arange(TOK_DEV), side="right"))(jax.random.split(seeds[4], BLOCKS)).reshape((BLOCKS, TOK_DEV)).astype(jnp.int32)
    cart_keys = draw_cart_keys(jax.random.fold_in(seeds[7], 71), 0)
    cart_values = noise(seeds[6], (CART, HK * HD), 1.0, 5.0, ((0, 32),))
    return {"queries": queries, "conv_keys": conv_keys, "conv_values": conv_values, "out_grad": out_grad, "segment_ids": segment_ids, "cart_keys": cart_keys, "cart_values": cart_values}


def block_terms(queries, conv_keys, conv_values, out_grad, segments, cart_keys, cart_values):
    scale = 1.0 / math.sqrt(HD)
    group = HQ // HK
    position = jnp.arange(TOK_DEV)
    allowed = (segments[:, None] == segments[None, :]) & (position[None, :] <= position[:, None])
    key_parts = []
    value_parts = []
    for head_group in range(HK):
        low = head_group * group * HD
        high = (head_group + 1) * group * HD
        query_group = queries[:, low:high].reshape(TOK_DEV, group, HD).astype(jnp.float32)
        grad_group = out_grad[:, low:high].reshape(TOK_DEV, group, HD).astype(jnp.float32)
        cols = slice(head_group * HD, (head_group + 1) * HD)
        cart_key = cart_keys[:, cols].astype(jnp.float32)
        cart_value = cart_values[:, cols].astype(jnp.float32)
        conv_key = conv_keys[:, cols].astype(jnp.float32)
        conv_value = conv_values[:, cols].astype(jnp.float32)
        score_cart = jnp.einsum('tgd,jd->tgj', query_group, cart_key) * scale
        score_conv = jnp.einsum('tgd,ud->tgu', query_group, conv_key) * scale
        score_conv = jnp.where(allowed[:, None, :], score_conv, -jnp.inf)
        top = jnp.maximum(lax.optimization_barrier(jnp.max(score_cart, axis=-1)), lax.optimization_barrier(jnp.max(score_conv, axis=-1)))
        exp_cart = jnp.exp(score_cart - top[..., None])
        exp_conv = jnp.exp(score_conv - top[..., None])
        total = lax.optimization_barrier(jnp.sum(exp_cart, axis=-1)) + lax.optimization_barrier(jnp.sum(exp_conv, axis=-1))
        probs_cart = exp_cart / total[..., None]
        probs_conv = exp_conv / total[..., None]
        rounded_cart = probs_cart.astype(jnp.bfloat16).astype(jnp.float32)
        rounded_conv = probs_conv.astype(jnp.bfloat16).astype(jnp.float32)
        mixed = jnp.einsum('tgj,jd->tgd', rounded_cart, cart_value) + jnp.einsum('tgu,ud->tgd', rounded_conv, conv_value)
        delta = lax.optimization_barrier(jnp.sum(grad_group * mixed, axis=-1))
        dprob = jnp.einsum('tgd,jd->tgj', grad_group, cart_value)
        dscore = probs_cart * (dprob - delta[..., None])
        dscore_b = dscore.astype(jnp.bfloat16).astype(jnp.float32)
        value_parts.append(jnp.einsum('tgj,tgd->jd', rounded_cart, grad_group))
        key_parts.append(jnp.einsum('tgj,tgd->jd', dscore_b, query_group) * scale)
    return jnp.concatenate(key_parts + value_parts, axis=1)

def reference(queries, conv_keys, conv_values, out_grad, segment_ids, cart_keys, cart_values):
    items = (queries.reshape(BLOCKS, TOK_DEV, HQ * HD), conv_keys.reshape(BLOCKS, TOK_DEV, HK * HD), conv_values.reshape(BLOCKS, TOK_DEV, HK * HD), out_grad.reshape(BLOCKS, TOK_DEV, HQ * HD), segment_ids)

    def step(carry, block):
        return (carry + block_terms(block[0], block[1], block[2], block[3], block[4], cart_keys, cart_values), None)
    start = jnp.zeros((CART, 2 * HK * HD), jnp.float32)
    summed = lax.scan(step, start, items)[0]
    return (summed[:, :HK * HD], summed[:, HK * HD:])
```

```python
import math

import jax
import jax.numpy as jnp
from jax import lax
from jax.experimental import pallas as pl
from jax.experimental.pallas import tpu as pltpu
from jax.sharding import PartitionSpec as P

HD = 128
TOK = 256
CART = 1024
HK = 4
GROUP = 8
HP = 2
CHUNK = 256
SCALE = 1.0 / math.sqrt(HD)
SCALE2 = SCALE * math.log2(math.e)
MASKED = -1e30

f32 = jnp.float32
bf16 = jnp.bfloat16
NT = (((1,), (1,)), ((), ()))
NN = (((1,), (0,)), ((), ()))


def dot(a, b, dims):
    return lax.dot_general(a, b, dims, preferred_element_type=f32)


def head_step(q, g, k_ref, v_ref, conv_k, conv_v, bias, acc):
    rows3 = lambda x: x.reshape(-1, 8, TOK)
    top = total = mixed = None
    held = []
    for c in range(-1, CART // CHUNK):
        if c < 0:
            s = rows3(dot(conv_k, q, NT) * SCALE2 + bias)
            dp = rows3(dot(conv_v, g, NT))
        else:
            rows = pl.ds(c * CHUNK, CHUNK)
            s = rows3(dot(k_ref[rows, :], q, NT) * SCALE2)
            dp = rows3(dot(v_ref[rows, :], g, NT))
        new = jnp.max(s, axis=0)
        if top is not None:
            new = jnp.maximum(top, new)
        e = jnp.exp2(s - new[None])
        part = jnp.sum(e, axis=0)
        mpart = jnp.sum(e * dp, axis=0)
        if top is not None:
            old = jnp.exp2(top - new)
            part = part + total * old
            mpart = mpart + mixed * old
        top, total, mixed = new, part, mpart
        if c >= 0:
            held.append((e, dp, top))
    last = jnp.max(top, axis=0, keepdims=True)
    fix = jnp.exp2(top - last)
    inv = 1.0 / jnp.sum(total * fix, axis=0, keepdims=True)
    delta = jnp.sum(mixed * fix, axis=0, keepdims=True) * inv
    for c, (e, dp, top) in enumerate(held):
        rows = pl.ds(c * CHUNK, CHUNK)
        p = e * (jnp.exp2(top - last) * inv)[None]
        ds = (p * (dp - delta[None])).reshape(CHUNK, TOK).astype(bf16)
        pb = p.reshape(CHUNK, TOK).astype(bf16)
        acc[rows, :HD] += dot(ds, q, NN)
        acc[rows, HD:] += dot(pb, g, NN)


def kernel(seg_row, seg_col, q_ref, g_ref, k_ref, v_ref, ck_ref, cv_ref, own_ref, sent_ref, acc, bias):
    group, step = pl.program_id(0), pl.program_id(1)

    @pl.when(jnp.logical_and(group == 0, step == 0))
    def _():
        key_at = lax.broadcasted_iota(jnp.int32, (TOK, TOK), 0)
        tok_at = lax.broadcasted_iota(jnp.int32, (TOK, TOK), 1)
        ok = (seg_col[...] == seg_row[...]) & (key_at <= tok_at)
        bias[...] = jnp.where(ok, 0.0, MASKED)

    @pl.when(step == 0)
    def _():
        acc[...] = jnp.zeros_like(acc)

    for j in range(HP):
        cols = slice(j * HD, (j + 1) * HD)
        head_step(q_ref[:, cols], g_ref[:, cols], k_ref, v_ref, ck_ref[...], cv_ref[...], bias[...], acc)

    @pl.when(step == GROUP // HP - 1)
    def _():
        half = CART // 2
        own_ref[:, :HD] = acc[:half, :HD] * SCALE
        own_ref[:, HD:] = acc[:half, HD:]
        sent_ref[:, :HD] = (acc[half:, :HD] * SCALE).astype(bf16)
        sent_ref[:, HD:] = acc[half:, HD:].astype(bf16)


def attention(segments, queries, out_grad, rows, conv_keys, conv_values):
    steps = GROUP // HP
    spec = pl.BlockSpec
    return pl.pallas_call(
        kernel,
        grid=(HK, steps),
        in_specs=[
            spec((1, TOK), lambda i, h: (0, 0)),
            spec((TOK, 1), lambda i, h: (0, 0)),
            spec((TOK, HP * HD), lambda i, h: (0, i * steps + h)),
            spec((TOK, HP * HD), lambda i, h: (0, i * steps + h)),
            spec((CART, HD), lambda i, h: (0, i)),
            spec((CART, HD), lambda i, h: (0, HK + i)),
            spec((TOK, HD), lambda i, h: (0, i)),
            spec((TOK, HD), lambda i, h: (0, i)),
        ],
        out_specs=[
            spec((CART // 2, 2 * HD), lambda i, h: (0, i)),
            spec((CART // 2, 2 * HD), lambda i, h: (0, i)),
        ],
        out_shape=[
            jax.ShapeDtypeStruct((CART // 2, 2 * HK * HD), f32),
            jax.ShapeDtypeStruct((CART // 2, 2 * HK * HD), bf16),
        ],
        scratch_shapes=[pltpu.VMEM((CART, 2 * HD), f32), pltpu.VMEM((TOK, TOK), f32)],
        compiler_params=pltpu.CompilerParams(vmem_limit_bytes=48 * 2**20),
    )(segments, segments.reshape(TOK, 1), queries, out_grad, rows, rows, conv_keys, conv_values)


CORE = [(i, i ^ 1) for i in range(32)]
XLO = [(i, i ^ 2) for i in range(32)]


def along_z(k):
    return [(z * 4 + r, ((z + k) % 8) * 4 + r) for z in range(8) for r in range(4)]


def per_device(queries, conv_keys, conv_values, out_grad, segment_ids, cart_keys, cart_values):
    own = jnp.concatenate([cart_keys, cart_values], axis=1)
    rows = jnp.concatenate([own] + [lax.ppermute(own, "ctx", along_z(k)) for k in range(1, 8)], axis=0)
    rows = jnp.concatenate([rows, lax.ppermute(rows, "ctx", XLO)], axis=0)
    rows = jnp.concatenate([rows, lax.ppermute(rows, "ctx", CORE)], axis=0)
    kept, sent = attention(segment_ids, queries, out_grad, rows, conv_keys, conv_values)
    part = kept + lax.ppermute(sent, "ctx", CORE).astype(f32)
    part = part[:256] + lax.ppermute(part[256:].astype(bf16), "ctx", XLO).astype(f32)
    sent = part[32:].astype(bf16)
    total = part[:32]
    for k in range(1, 8):
        total = total + lax.ppermute(sent[(k - 1) * 32 : k * 32], "ctx", along_z(-k)).astype(f32)
    parts = [lax.ppermute(total, "dp", [(i, i ^ k) for i in range(8)]) for k in range(1, 8)]
    level = [total] + parts
    while len(level) > 1:
        level = [level[j] + level[j + 1] for j in range(0, len(level), 2)]
    summed = level[0]
    summed = summed.reshape(32, HK, 2, HD)
    return summed[:, :, 0].reshape(32, HK * HD), summed[:, :, 1].reshape(32, HK * HD)


def solution(mesh):
    every = P(("dp", "ctx"), None)
    return jax.shard_map(
        per_device,
        mesh=mesh,
        in_specs=(every,) * 5 + (P("ctx", None),) * 2,
        out_specs=(P("ctx", None),) * 2,
        check_vma=False,
    )
```
